32 devices in a mesh: member: 8 (over z, y), fsdp: 4 (over x, core).
Axes of the slice: x: 2, y: 2, z: 4, core: 2. Of those that a mesh axis runs over, the one named last changes fastest.
Arguments:
- probe_acts: bfloat16 [8, 4, 224, 4096], P('member', 'fsdp'), may hold values from -6 to 6
- member_weight: bfloat16 [8, 4096, 1792], P('member', 'fsdp'), may hold values from -6 to 6
- gate_values: bfloat16 [8, 4, 224, 1792], P('member', 'fsdp'), may hold values from -6 to 6
- out_grad: bfloat16 [8, 4, 224, 1792], P('member', 'fsdp'), may hold values from -6 to 6
- loss_mask: int32 [4, 224], P('fsdp'), may hold values 0 or 1
Outputs:
- merged: bfloat16 [4096, 1792], P(None, 'member')
- fisher_mean: float32 [4096, 1792], P('fsdp', 'member')
The draws below stay inside these ranges and needn't reach their ends.
All inputs are finite; a program needn't handle non-finite values. No bound on the sum of `loss_mask` on one device may be relied on, other than what follows from the above.
Results may differ from the reference program's by a relative error of at most 0.0045.
Values may be sent and summed in bfloat16 or wider, within the bound.
A program may use at most 128 MiB of HBM per device.

```python
import jax
import jax.numpy as jnp
from jax import lax

D = 4096
COLS = 1792
LEN = 224
MEMBERS = 8
EXAMPLES = 4


def with_ends(drawn, own_key, least, high):
    spot = [jax.random.randint(jax.random.fold_in(own_key, axis), (), 0, length) for axis, length in enumerate(drawn.shape)]
    widest = drawn.shape.index(max(drawn.shape))
    beside = spot[:widest] + [(spot[widest] + 1) % drawn.shape[widest]] + spot[widest + 1:]
    return drawn.at[tuple(spot)].set(least).at[tuple(beside)].set(high)


def levels(rng, dims, shards, least, largest):
    level, own = 1.0, jax.random.fold_in(rng, 6)
    for position, blocks in shards:
        steps = jnp.exp(jax.random.uniform(jax.random.fold_in(own, position), (blocks,), jnp.float32, least / len(shards), largest / len(shards)))
        level = level * jnp.repeat(steps, dims[position] // blocks).reshape([-1 if axis == position else 1 for axis in range(len(dims))])
    return level


def normal_values(rng, extent, spread, bound, split=(), dtype=jnp.bfloat16):
    loudness = levels(rng, extent, split, -0.22, 0.18) if split else 1.0
    drawn = jax.random.normal(rng, extent, jnp.float32) * spread * loudness
    return jnp.minimum(jnp.maximum(drawn, -bound), bound).astype(dtype)


def setup_inputs(seed: int = 0) -> dict:
    keys = jax.random.split(jax.random.key(seed), 6)
    return {
        "probe_acts": normal_values(keys[0], (MEMBERS, EXAMPLES, LEN, D), 1.0, 6.0, ((0, 8), (1, 4))),
        "member_weight": normal_values(keys[1], (MEMBERS, D, COLS), 1.0, 6.0, ((0, 8), (1, 4))),
        "gate_values": normal_values(keys[2], (MEMBERS, EXAMPLES, LEN, COLS), 1.0, 6.0, ((0, 8), (1, 4))),
        "out_grad": normal_values(keys[3], (MEMBERS, EXAMPLES, LEN, COLS), 1.0, 6.0, ((0, 8), (1, 4))),
        "loss_mask": with_ends((jax.random.randint(keys[4], (EXAMPLES, LEN), 0, 4) < 3).astype(jnp.int32), jax.random.fold_in(keys[4], 1), 0, 1),
    }


def reference(probe_acts, member_weight, gate_values, out_grad, loss_mask):
    mask_float = loss_mask.astype(jnp.float32)[:, :, None]

    def one_member(carry, inputs):
        fisher_total, weighted = carry
        acts_member, weight_member, gate_member, grad_member = inputs
        gate_act = jax.nn.silu(gate_member.astype(jnp.float32))
        cotangent = (mask_float * grad_member.astype(jnp.float32) * gate_act).astype(jnp.bfloat16)

        def add_example(total, pair):
            acts_one, cot_one = pair
            grads = jnp.einsum('ld,lc->dc', acts_one.astype(jnp.float32), cot_one.astype(jnp.float32))
            return total + grads * grads, None

        squares, unused = lax.scan(add_example, jnp.zeros((D, COLS), jnp.float32), (acts_member, cotangent))
        fisher = squares / (EXAMPLES * LEN)
        return (fisher_total + fisher, weighted + fisher * weight_member.astype(jnp.float32)), None

    start = (jnp.zeros((D, COLS), jnp.float32), jnp.zeros((D, COLS), jnp.float32))
    (fisher_total, weighted), unused = lax.scan(one_member, start, (probe_acts, member_weight, gate_values, out_grad))
    merged = (weighted / (fisher_total + 1e-6)).astype(jnp.bfloat16)
    fisher_mean = fisher_total / MEMBERS
    return merged, fisher_mean
```

```python
import functools

import jax
import jax.numpy as jnp
from jax import lax
from jax.experimental import pallas as pl
from jax.experimental.pallas import tpu as pltpu
from jax.sharding import PartitionSpec as P

MESH = pl.DeviceIdType.MESH
F32 = jnp.float32
BF16 = jnp.bfloat16


def merge_kernel(
    F, M, C, acts_hbm, w_hbm, gate, grad, mask, merged_out, fisher_out,
    acts, cots, cot_t, w, w_t, ysend, yrecv, zsend, zrecv, own, fin, fmean,
    acts_ss, acts_rs, acts_ls, cot_ss, cot_rs, w_ls, y_ss, y_rs, z_ss, z_rs, fin_ss, fin_rs, out_ls,
):
    f = lax.axis_index("fsdp")
    m = lax.axis_index("member")
    Z = M // 2
    z = lax.div(m, 2)
    y = lax.rem(m, 2)
    L = cots.shape[2]
    H = cots.shape[3]
    COLS = 2 * H
    S = COLS // M
    CH = acts.shape[3]
    R = C * CH
    norm = 1.0 / (F * L)
    mate = f + 1 - 2 * lax.rem(f, 2)
    m_y = m + 1 - 2 * y

    def peer(d):
        return lax.rem(f + d, F)

    barrier = pltpu.get_barrier_semaphore()
    for d in range(1, F):
        pl.semaphore_signal(barrier, inc=1, device_id=(m, peer(d)), device_id_type=MESH)
    pl.semaphore_signal(barrier, inc=1, device_id=(m_y, f), device_id_type=MESH)

    @pl.when(z > 0)
    def _():
        pl.semaphore_signal(barrier, inc=1, device_id=(m - 2, f), device_id_type=MESH)

    @pl.when(z < Z - 1)
    def _():
        pl.semaphore_signal(barrier, inc=1, device_id=(m + 2, f), device_id_type=MESH)

    w_copy = pltpu.make_async_copy(w_hbm, w, w_ls)
    w_copy.start()

    def own_acts(c):
        start = pl.multiple_of(f * R + c * CH, 128)
        return pltpu.make_async_copy(acts_hbm.at[:, pl.ds(start, CH)], acts.at[c, f], acts_ls.at[c])

    for c in range(C):
        own_acts(c).start()

    def acts_copy(d, c):
        p = peer(d)
        start = pl.multiple_of(p * R + c * CH, 128)
        return pltpu.make_async_remote_copy(
            src_ref=acts_hbm.at[:, pl.ds(start, CH)], dst_ref=acts.at[c, f],
            send_sem=acts_ss.at[d - 1, c], recv_sem=acts_rs.at[f, c],
            device_id=(m, p), device_id_type=MESH)

    def acts_arrival(d, c):
        s = peer(d)
        return pltpu.make_async_remote_copy(
            src_ref=acts.at[c, s], dst_ref=acts.at[c, s],
            send_sem=acts_ss.at[d - 1, c], recv_sem=acts_rs.at[s, c],
            device_id=(m, s), device_id_type=MESH)

    def cot_copy(s, h, p, slot):
        return pltpu.make_async_remote_copy(
            src_ref=cots.at[h, s], dst_ref=cots.at[h, s],
            send_sem=cot_ss.at[slot, h], recv_sem=cot_rs.at[s, h],
            device_id=(m, p), device_id_type=MESH)

    lower = z < Z // 2
    first = jnp.where(lower, 1, 0)
    second = 1 - first

    mask_col = jnp.transpose(jnp.broadcast_to(mask[...].astype(F32), (128, L)))

    def make_cot(h):
        for t in range(H // 128):
            cols = pl.ds(pl.multiple_of(h * H + t * 128, 128), 128)
            g = gate[:, cols].astype(F32)
            value = mask_col * grad[:, cols].astype(F32) * (g / (1.0 + jnp.exp(-g)))
            cots[h, f, :, t * 128:(t + 1) * 128] = value.astype(BF16)

    def send_cot(h):
        for d in range(2, F, 2):
            cot_copy(f, h, peer(d), d).start()
        cot_copy(f, h, mate, 0).start()

    make_cot(first)
    pl.semaphore_wait(barrier, F + jnp.where(z > 0, 1, 0) + jnp.where(z < Z - 1, 1, 0))

    send_cot(first)
    for d in range(1, F):
        acts_copy(d, 0).start()
    make_cot(second)
    send_cot(second)
    for c in range(1, C):
        for d in range(1, F):
            acts_copy(d, c).start()

    w_copy.wait()

    def turn_weight(c, carry):
        rows = pl.ds(pl.multiple_of(c * CH, CH), CH)
        for t in range(COLS // 128):
            tile = w[rows, t * 128:(t + 1) * 128].astype(F32)
            w_t[c, t * 128:(t + 1) * 128, :] = jnp.transpose(tile)
        return carry

    lax.fori_loop(0, C, turn_weight, 0)

    def relay(h):
        for d in range(2, F, 2):
            s = peer(d)
            cot_copy(s, h, s, d).wait_recv()
            cot_copy(s, h, mate, d + 1).start()

    def turn_cot(h):
        for d in range(1, F, 2):
            s = peer(d)
            cot_copy(s, h, s, d).wait_recv()

        def one(e, carry):
            for t in range(H // 128):
                tile = cots[h, e, :, t * 128:(t + 1) * 128].astype(F32)
                rows = pl.ds(pl.multiple_of(h * H + t * 128, 128), 128)
                cot_t[e, rows, :] = jnp.transpose(tile)
            return carry

        lax.fori_loop(0, F, one, 0)

    relay(first)

    def share(j, c):
        rows = pl.ds(pl.multiple_of(j * S, 8), S)
        squares = None
        for e in range(F):
            g = jnp.dot(cot_t[e, rows, :].astype(BF16), acts[c, e], preferred_element_type=F32)
            squares = g * g if squares is None else squares + g * g
        fisher = squares * norm
        return fisher, fisher * w_t[c, rows, :]

    def y_copy(c, k):
        return pltpu.make_async_remote_copy(
            src_ref=ysend.at[c, k], dst_ref=yrecv.at[c, k],
            send_sem=y_ss.at[c, k], recv_sem=y_rs.at[c, k],
            device_id=(m_y, f), device_id_type=MESH)

    def z_copy(c, k, slot, target):
        return pltpu.make_async_remote_copy(
            src_ref=zsend.at[c, k], dst_ref=zrecv.at[c, slot],
            send_sem=z_ss.at[c, k], recv_sem=z_rs.at[c, slot],
            device_id=(target, f), device_id_type=MESH)

    def fin_copy(c, d):
        return pltpu.make_async_remote_copy(
            src_ref=fin.at[c], dst_ref=merged_out.at[f, :, pl.ds(pl.multiple_of(c * CH, CH), CH)],
            send_sem=fin_ss.at[d, c], recv_sem=fin_rs.at[f, c],
            device_id=(m, peer(d)), device_id_type=MESH)

    def fin_arrival(c, d):
        s = peer(d)
        return pltpu.make_async_remote_copy(
            src_ref=fin.at[c], dst_ref=merged_out.at[s, :, pl.ds(pl.multiple_of(c * CH, CH), CH)],
            send_sem=fin_ss.at[d, c], recv_sem=fin_rs.at[s, c],
            device_id=(m, s), device_id_type=MESH)

    def out_copies(c):
        cols = pl.ds(pl.multiple_of(c * CH, CH), CH)
        return (
            pltpu.make_async_copy(fin.at[c], merged_out.at[f, :, cols], out_ls.at[0, c]),
            pltpu.make_async_copy(fmean.at[c], fisher_out.at[:, cols], out_ls.at[1, c]),
        )

    def combine(c, k):
        b = lax.rem(c, 2)
        y_copy(c, k).wait_recv()
        own[b, k] = own[b, k] + yrecv[c, k].astype(F32)

        @pl.when((z > 0) & (k >= z))
        def _():
            z_copy(c, k, k, m_y).wait_recv()
            own[b, k] = own[b, k] + zrecv[c, k].astype(F32)

        @pl.when((z < Z - 1) & (k <= z))
        def _():
            slot = jnp.where(k == z, Z, k)
            z_copy(c, k, slot, m_y).wait_recv()
            own[b, k] = own[b, k] + zrecv[c, slot].astype(F32)

        @pl.when(k != z)
        def _():
            zsend[c, k] = own[b, k].astype(BF16)

        @pl.when(k > z)
        def _():
            z_copy(c, k, k, m + 2).start()

        @pl.when(k < z)
        def _():
            z_copy(c, k, jnp.where(k == z - 1, Z, k), m - 2).start()

        @pl.when(k == z)
        def _():
            total = own[b, k, 0]
            fin[c] = (own[b, k, 1] / (total + 1e-6)).astype(BF16)
            fmean[c] = total * (1.0 / M)
            for d in range(1, F):
                fin_copy(c, d).start()
            for copy in out_copies(c):
                copy.start()

    def order(i):
        return jnp.where(lower, Z - 1 - i, i)

    def step(t, carry):
        c = lax.div(t, Z)
        i = lax.rem(t, Z)
        k = order(i)

        @pl.when(t == 0)
        def _():
            turn_cot(first)

        @pl.when(t == 1)
        def _():
            relay(second)

        @pl.when(t == Z // 2)
        def _():
            turn_cot(second)

        @pl.when((i == 0) & (c < C))
        def _():
            own_acts(c).wait()
            for d in range(1, F):
                acts_arrival(d, c).wait_recv()

        @pl.when(c < C)
        def _():
            fisher, weighted = share(2 * k + 1 - y, c)
            ysend[c, k, 0] = fisher.astype(BF16)
            ysend[c, k, 1] = weighted.astype(BF16)
            y_copy(c, k).start()

        @pl.when(c > 0)
        def _():
            combine(c - 1, k)

        @pl.when(c < C)
        def _():
            fisher, weighted = share(2 * k + y, c)
            b = lax.rem(c, 2)
            own[b, k, 0] = fisher
            own[b, k, 1] = weighted

        return carry

    lax.fori_loop(0, (C + 1) * Z, step, 0)

    for h in range(2):
        for slot in [0] + [s for d in range(2, F, 2) for s in (d, d + 1)]:
            cot_copy(f, h, mate, slot).wait_send()

    def drain(c, carry):
        for d in range(1, F):
            acts_copy(d, c).wait_send()
            fin_copy(c, d).wait_send()
            fin_arrival(c, d).wait_recv()
        for copy in out_copies(c):
            copy.wait()

        def drain_k(k, carry):
            y_copy(c, k).wait_send()

            @pl.when(k != z)
            def _():
                z_copy(c, k, k, m_y).wait_send()

            return carry

        return lax.fori_loop(0, Z, drain_k, carry)

    lax.fori_loop(0, C, drain, 0)


def shards(F, M, probe_acts, member_weight, gate_values, out_grad, loss_mask):
    acts = probe_acts[0, 0]
    weight = member_weight[0]
    gate = gate_values[0, 0]
    grad = out_grad[0, 0]
    L, D = acts.shape
    R, COLS = weight.shape
    S = COLS // M
    Z = M // 2
    CH = max(128, R // 4)
    C = R // CH
    dma = pltpu.SemaphoreType.DMA
    vmem = pl.BlockSpec(memory_space=pltpu.VMEM)
    hbm = pl.BlockSpec(memory_space=pl.ANY)
    merged, fisher = pl.pallas_call(
        functools.partial(merge_kernel, F, M, C),
        out_shape=(
            jax.ShapeDtypeStruct((F, S, R), BF16),
            jax.ShapeDtypeStruct((S, R), F32),
        ),
        in_specs=[hbm, hbm, vmem, vmem, vmem],
        out_specs=(hbm, hbm),
        scratch_shapes=[
            pltpu.VMEM((C, F, L, CH), BF16),
            pltpu.VMEM((2, F, L, COLS // 2), BF16),
            pltpu.VMEM((F, COLS, L), F32),
            pltpu.VMEM((R, COLS), BF16),
            pltpu.VMEM((C, COLS, CH), F32),
            pltpu.VMEM((C, Z, 2, S, CH), BF16),
            pltpu.VMEM((C, Z, 2, S, CH), BF16),
            pltpu.VMEM((C, Z, 2, S, CH), BF16),
            pltpu.VMEM((C, Z + 1, 2, S, CH), BF16),
            pltpu.VMEM((2, Z, 2, S, CH), F32),
            pltpu.VMEM((C, S, CH), BF16),
            pltpu.VMEM((C, S, CH), F32),
            dma((F, C)), dma((F, C)), dma((C,)),
            dma((F, 2)), dma((F, 2)), dma,
            dma((C, Z)), dma((C, Z)),
            dma((C, Z)), dma((C, Z + 1)),
            dma((F, C)), dma((F, C)), dma((2, C)),
        ],
        compiler_params=pltpu.CompilerParams(
            collective_id=0, has_side_effects=True, vmem_limit_bytes=60 * 1024 * 1024),
        cost_estimate=pl.CostEstimate(
            flops=2 * F * L * R * COLS, bytes_accessed=2 * R * COLS, transcendentals=L * COLS),
    )(acts, weight, gate, grad, loss_mask)
    merged = jnp.transpose(merged, (0, 2, 1)).reshape(F * R, S)
    return merged, jnp.transpose(fisher)


def solution(mesh):
    in_specs = (
        P("member", "fsdp", None, None),
        P("member", "fsdp", None),
        P("member", "fsdp", None, None),
        P("member", "fsdp", None, None),
        P("fsdp", None),
    )
    out_specs = (P(None, "member"), P("fsdp", "member"))
    body = functools.partial(shards, mesh.shape["fsdp"], mesh.shape["member"])
    return jax.shard_map(body, mesh=mesh, in_specs=in_specs, out_specs=out_specs, check_vma=False)
```

```python
import functools

import jax
import jax.numpy as jnp
from jax import lax
from jax.experimental import pallas as pl
from jax.experimental.pallas import tpu as pltpu
from jax.sharding import PartitionSpec as P

MESH = pl.DeviceIdType.MESH
F32 = jnp.float32
BF16 = jnp.bfloat16
LAG = 3


def merge_kernel(
    F, M, C, acts_hbm, w_hbm, gate, grad, mask, merged_out, fisher_out,
    acts, cots, cot_t, w, w_t, ysend, yrecv, zsend, zrecv, own, fin, fmean,
    acts_ss, acts_rs, acts_ls, cot_ss, cot_rs, w_ls, y_ss, y_rs, z_ss, z_rs, fin_ss, fin_rs, out_ls,
):
    f = lax.axis_index("fsdp")
    m = lax.axis_index("member")
    Z = M // 2
    z = lax.div(m, 2)
    y = lax.rem(m, 2)
    L = cots.shape[2]
    H = cots.shape[3]
    COLS = 2 * H
    S = COLS // M
    CH = acts.shape[3]
    R = C * CH
    norm = 1.0 / (F * L)
    mate = f + 1 - 2 * lax.rem(f, 2)
    m_y = m + 1 - 2 * y

    def peer(d):
        return lax.rem(f + d, F)

    barrier = pltpu.get_barrier_semaphore()
    for d in range(1, F):
        pl.semaphore_signal(barrier, inc=1, device_id=(m, peer(d)), device_id_type=MESH)
    pl.semaphore_signal(barrier, inc=1, device_id=(m_y, f), device_id_type=MESH)

    @pl.when(z > 0)
    def _():
        pl.semaphore_signal(barrier, inc=1, device_id=(m - 2, f), device_id_type=MESH)

    @pl.when(z < Z - 1)
    def _():
        pl.semaphore_signal(barrier, inc=1, device_id=(m + 2, f), device_id_type=MESH)

    w_copy = pltpu.make_async_copy(w_hbm, w, w_ls)
    w_copy.start()

    def own_acts(c):
        start = pl.multiple_of(f * R + c * CH, 128)
        return pltpu.make_async_copy(acts_hbm.at[:, pl.ds(start, CH)], acts.at[c, f], acts_ls.at[c])

    for c in range(C):
        own_acts(c).start()

    def acts_copy(d, c):
        p = peer(d)
        start = pl.multiple_of(p * R + c * CH, 128)
        return pltpu.make_async_remote_copy(
            src_ref=acts_hbm.at[:, pl.ds(start, CH)], dst_ref=acts.at[c, f],
            send_sem=acts_ss.at[d - 1, c], recv_sem=acts_rs.at[f, c],
            device_id=(m, p), device_id_type=MESH)

    def acts_arrival(d, c):
        s = peer(d)
        return pltpu.make_async_remote_copy(
            src_ref=acts.at[c, s], dst_ref=acts.at[c, s],
            send_sem=acts_ss.at[d - 1, c], recv_sem=acts_rs.at[s, c],
            device_id=(m, s), device_id_type=MESH)

    def cot_copy(s, h, p, slot):
        return pltpu.make_async_remote_copy(
            src_ref=cots.at[h, s], dst_ref=cots.at[h, s],
            send_sem=cot_ss.at[slot, h], recv_sem=cot_rs.at[s, h],
            device_id=(m, p), device_id_type=MESH)

    lower = z < Z // 2
    first = jnp.where(lower, 1, 0)
    second = 1 - first

    mask_col = jnp.transpose(jnp.broadcast_to(mask[...].astype(F32), (128, L)))

    def make_cot(h):
        for t in range(H // 128):
            cols = pl.ds(pl.multiple_of(h * H + t * 128, 128), 128)
            g = gate[:, cols].astype(F32)
            value = mask_col * grad[:, cols].astype(F32) * (g / (1.0 + jnp.exp(-g)))
            cots[h, f, :, t * 128:(t + 1) * 128] = value.astype(BF16)

    def send_cot(h):
        for d in range(2, F, 2):
            cot_copy(f, h, peer(d), d).start()
        cot_copy(f, h, mate, 0).start()

    make_cot(first)
    pl.semaphore_wait(barrier, F + jnp.where(z > 0, 1, 0) + jnp.where(z < Z - 1, 1, 0))

    send_cot(first)
    for d in range(1, F):
        acts_copy(d, 0).start()
    make_cot(second)
    send_cot(second)
    for c in range(1, C):
        for d in range(1, F):
            acts_copy(d, c).start()

    w_copy.wait()

    def turn_weight(c, carry):
        rows = pl.ds(pl.multiple_of(c * CH, CH), CH)
        for t in range(COLS // 128):
            tile = w[rows, t * 128:(t + 1) * 128].astype(F32)
            w_t[c, t * 128:(t + 1) * 128, :] = jnp.transpose(tile)
        return carry

    lax.fori_loop(0, C, turn_weight, 0)

    def relay(h):
        for d in range(2, F, 2):
            s = peer(d)
            cot_copy(s, h, s, d).wait_recv()
            cot_copy(s, h, mate, d + 1).start()

    def turn_cot(h):
        for d in range(1, F, 2):
            s = peer(d)
            cot_copy(s, h, s, d).wait_recv()

        def one(e, carry):
            for t in range(H // 128):
                tile = cots[h, e, :, t * 128:(t + 1) * 128].astype(F32)
                rows = pl.ds(pl.multiple_of(h * H + t * 128, 128), 128)
                cot_t[e, rows, :] = jnp.transpose(tile)
            return carry

        lax.fori_loop(0, F, one, 0)

    relay(first)

    def share(j, c):
        rows = pl.ds(pl.multiple_of(j * S, 8), S)
        squares = None
        for e in range(F):
            g = jnp.dot(cot_t[e, rows, :].astype(BF16), acts[c, e], preferred_element_type=F32)
            squares = g * g if squares is None else squares + g * g
        fisher = squares * norm
        return fisher, fisher * w_t[c, rows, :]

    def y_copy(c, k):
        return pltpu.make_async_remote_copy(
            src_ref=ysend.at[c, k], dst_ref=yrecv.at[c, k],
            send_sem=y_ss.at[c, k], recv_sem=y_rs.at[c, k],
            device_id=(m_y, f), device_id_type=MESH)

    def z_copy(c, k, slot, target):
        return pltpu.make_async_remote_copy(
            src_ref=zsend.at[c, k], dst_ref=zrecv.at[c, slot],
            send_sem=z_ss.at[c, k], recv_sem=z_rs.at[c, slot],
            device_id=(target, f), device_id_type=MESH)

    def fin_copy(c, d):
        return pltpu.make_async_remote_copy(
            src_ref=fin.at[c], dst_ref=merged_out.at[f, :, pl.ds(pl.multiple_of(c * CH, CH), CH)],
            send_sem=fin_ss.at[d, c], recv_sem=fin_rs.at[f, c],
            device_id=(m, peer(d)), device_id_type=MESH)

    def fin_arrival(c, d):
        s = peer(d)
        return pltpu.make_async_remote_copy(
            src_ref=fin.at[c], dst_ref=merged_out.at[s, :, pl.ds(pl.multiple_of(c * CH, CH), CH)],
            send_sem=fin_ss.at[d, c], recv_sem=fin_rs.at[s, c],
            device_id=(m, s), device_id_type=MESH)

    def out_copies(c):
        cols = pl.ds(pl.multiple_of(c * CH, CH), CH)
        return (
            pltpu.make_async_copy(fin.at[c], merged_out.at[f, :, cols], out_ls.at[0, c]),
            pltpu.make_async_copy(fmean.at[c], fisher_out.at[:, cols], out_ls.at[1, c]),
        )

    def combine(c, k):
        b = lax.rem(c, 2)
        y_copy(c, k).wait_recv()
        own[b, k] = own[b, k] + yrecv[c, k].astype(F32)

        @pl.when((z > 0) & (k >= z))
        def _():
            z_copy(c, k, k, m_y).wait_recv()
            own[b, k] = own[b, k] + zrecv[c, k].astype(F32)

        @pl.when((z < Z - 1) & (k <= z))
        def _():
            slot = jnp.where(k == z, Z, k)
            z_copy(c, k, slot, m_y).wait_recv()
            own[b, k] = own[b, k] + zrecv[c, slot].astype(F32)

        @pl.when(k != z)
        def _():
            zsend[c, k] = own[b, k].astype(BF16)

        @pl.when(k > z)
        def _():
            z_copy(c, k, k, m + 2).start()

        @pl.when(k < z)
        def _():
            z_copy(c, k, jnp.where(k == z - 1, Z, k), m - 2).start()

        @pl.when(k == z)
        def _():
            total = own[b, k, 0]
            fin[c] = (own[b, k, 1] / (total + 1e-6)).astype(BF16)
            fmean[c] = total * (1.0 / M)
            for d in range(1, F):
                fin_copy(c, d).start()
            for copy in out_copies(c):
                copy.start()

    def order(i):
        return jnp.where(lower, Z - 1 - i, i)

    def step(t, carry):
        c = lax.div(t, Z)
        i = lax.rem(t, Z)
        k = order(i)

        @pl.when(t == 0)
        def _():
            turn_cot(first)

        @pl.when(t == 1)
        def _():
            relay(second)

        @pl.when(t == Z // 2)
        def _():
            turn_cot(second)

        @pl.when((i == 0) & (c < C))
        def _():
            own_acts(c).wait()
            for d in range(1, F):
                acts_arrival(d, c).wait_recv()

        @pl.when(c < C)
        def _():
            fisher, weighted = share(2 * k + 1 - y, c)
            ysend[c, k, 0] = fisher.astype(BF16)
            ysend[c, k, 1] = weighted.astype(BF16)
            y_copy(c, k).start()

        @pl.when(c < C)
        def _():
            fisher, weighted = share(2 * k + y, c)
            b = lax.rem(c, 2)
            own[b, k, 0] = fisher
            own[b, k, 1] = weighted

        @pl.when(t >= LAG)
        def _():
            late = t - LAG
            k_late = order(lax.rem(late, Z))
            c_late = lax.div(late, Z) - jnp.where(k_late == z, 1, 0)

            @pl.when(c_late >= 0)
            def _():
                combine(c_late, k_late)

        return carry

    lax.fori_loop(0, C * Z + LAG, step, 0)
    combine(C - 1, z)

    for h in range(2):
        for slot in [0] + [s for d in range(2, F, 2) for s in (d, d + 1)]:
            cot_copy(f, h, mate, slot).wait_send()

    def drain(c, carry):
        for d in range(1, F):
            acts_copy(d, c).wait_send()
            fin_copy(c, d).wait_send()
            fin_arrival(c, d).wait_recv()
        for copy in out_copies(c):
            copy.wait()

        def drain_k(k, carry):
            y_copy(c, k).wait_send()

            @pl.when(k != z)
            def _():
                z_copy(c, k, k, m_y).wait_send()

            return carry

        return lax.fori_loop(0, Z, drain_k, carry)

    lax.fori_loop(0, C, drain, 0)


def shards(F, M, probe_acts, member_weight, gate_values, out_grad, loss_mask):
    acts = probe_acts[0, 0]
    weight = member_weight[0]
    gate = gate_values[0, 0]
    grad = out_grad[0, 0]
    L, D = acts.shape
    R, COLS = weight.shape
    S = COLS // M
    Z = M // 2
    CH = max(128, R // 4)
    C = R // CH
    dma = pltpu.SemaphoreType.DMA
    vmem = pl.BlockSpec(memory_space=pltpu.VMEM)
    hbm = pl.BlockSpec(memory_space=pl.ANY)
    merged, fisher = pl.pallas_call(
        functools.partial(merge_kernel, F, M, C),
        out_shape=(
            jax.ShapeDtypeStruct((F, S, R), BF16),
            jax.ShapeDtypeStruct((S, R), F32),
        ),
        in_specs=[hbm, hbm, vmem, vmem, vmem],
        out_specs=(hbm, hbm),
        scratch_shapes=[
            pltpu.VMEM((C, F, L, CH), BF16),
            pltpu.VMEM((2, F, L, COLS // 2), BF16),
            pltpu.VMEM((F, COLS, L), F32),
            pltpu.VMEM((R, COLS), BF16),
            pltpu.VMEM((C, COLS, CH), F32),
            pltpu.VMEM((C, Z, 2, S, CH), BF16),
            pltpu.VMEM((C, Z, 2, S, CH), BF16),
            pltpu.VMEM((C, Z, 2, S, CH), BF16),
            pltpu.VMEM((C, Z + 1, 2, S, CH), BF16),
            pltpu.VMEM((2, Z, 2, S, CH), F32),
            pltpu.VMEM((C, S, CH), BF16),
            pltpu.VMEM((C, S, CH), F32),
            dma((F, C)), dma((F, C)), dma((C,)),
            dma((F, 2)), dma((F, 2)), dma,
            dma((C, Z)), dma((C, Z)),
            dma((C, Z)), dma((C, Z + 1)),
            dma((F, C)), dma((F, C)), dma((2, C)),
        ],
        compiler_params=pltpu.CompilerParams(
            collective_id=0, has_side_effects=True, vmem_limit_bytes=60 * 1024 * 1024),
        cost_estimate=pl.CostEstimate(
            flops=2 * F * L * R * COLS, bytes_accessed=2 * R * COLS, transcendentals=L * COLS),
    )(acts, weight, gate, grad, loss_mask)
    merged = jnp.transpose(merged, (0, 2, 1)).reshape(F * R, S)
    return merged, jnp.transpose(fisher)


def solution(mesh):
    in_specs = (
        P("member", "fsdp", None, None),
        P("member", "fsdp", None),
        P("member", "fsdp", None, None),
        P("member", "fsdp", None, None),
        P("fsdp", None),
    )
    out_specs = (P(None, "member"), P("fsdp", "member"))
    body = functools.partial(shards, mesh.shape["fsdp"], mesh.shape["member"])
    return jax.shard_map(body, mesh=mesh, in_specs=in_specs, out_specs=out_specs, check_vma=False)
```
